512 devices in a mesh: dp: 128 (over z, y, core), mp: 4 (over x).
Axes of the slice: x: 4, y: 4, z: 16, core: 2. Of those that a mesh axis runs over, the one named last changes fastest.
Arguments:
- queries: bfloat16 [24576, 4096], P('dp', 'mp'), as said below
- passages: bfloat16 [8192, 4096], P('dp', 'mp'), as said below
- pair_block: int32 [128, 128], P(None, 'dp'), may hold values from 0 to 3
- positives: int32 [24576], P('dp'), may hold values from 0 to 2047
Outputs:
- loss: float32 [], replicated
- query_grad: float32 [24576, 4096], P('dp', 'mp')
- passage_grad: float32 [8192, 4096], P('dp', 'mp')
The draws below stay inside these ranges and needn't reach their ends.
Inputs may be any that keep to these rules, and one draw needn't show every extreme that they name: `queries`: query embeddings. `passages`: passage embeddings.
All inputs are finite; a program needn't handle non-finite values.
Results may differ from the reference program's by a relative error of at most 0.0019.
Values may be sent and summed in bfloat16 or wider, within the bound.
No kernel may reach another device: no remote copies, remote signals or barrier semaphores. Data moves between devices by JAX's collectives and lax.ppermute only.
A program may use at most 64 MiB of HBM per device.

```python
import math
import jax
import jax.numpy as jnp
import numpy as np
from jax import lax

D = 4096
QBLK = 192
PBLK = 16
PB_DEV = 4
QUERIES = 24576
PASSAGES = 8192
CANDS = 2048
N_DP = 128


def draw_queries(key, part):
    key = jax.random.fold_in(key, 3)
    first = jax.random.fold_in(key, 0)
    values = 0.177 * jax.random.normal(first, (QUERIES, D), jnp.float32)
    return values.astype(jnp.bfloat16)


def draw_passages(key, part):
    key = jax.random.fold_in(key, 5)
    first = jax.random.fold_in(key, 0)
    values = 0.177 * jax.random.normal(first, (PASSAGES, D), jnp.float32)
    return values.astype(jnp.bfloat16)


def set_ends(entries, rng, low, largest):
    spot = [jax.random.randint(jax.random.fold_in(rng, axis), (), 0, length) for axis, length in enumerate(entries.shape)]
    widest = entries.shape.index(max(entries.shape))
    neighbour = spot[:widest] + [(spot[widest] + 1) % entries.shape[widest]] + spot[widest + 1:]
    return entries.at[tuple(spot)].set(low).at[tuple(neighbour)].set(largest)


def cumulative_ranks(amount, slope):
    loads = [(1 << 20) // math.isqrt(rank ** slope) + 1 for rank in range(1, amount + 1)]
    width = 1 + sum(loads) // (1 << 30)
    return np.cumsum(np.array([max(1, weight // width) for weight in loads]))


def ranked(own_key, dims, amount, slope):
    listing = cumulative_ranks(amount, slope)
    pick = jax.random.randint(jax.random.fold_in(own_key, 1), dims, 0, int(listing[amount - 1]))
    standing = jnp.searchsorted(jnp.asarray(listing, jnp.int32), pick, side="right")
    return jax.random.permutation(jax.random.fold_in(own_key, 2), amount)[standing].astype(jnp.int32)


def setup_inputs(seed: int = 0) -> dict:
    key_of = jax.random.split(jax.random.key(seed), 5)
    queries = draw_queries(jax.random.fold_in(key_of[4], 71), 0)
    passages = draw_passages(jax.random.fold_in(key_of[4], 71), 0)
    pair_block = set_ends(ranked(key_of[2], (N_DP, N_DP), PB_DEV, 2), jax.random.fold_in(key_of[2], 3), 0, PB_DEV - 1).astype(jnp.int32)
    positives = set_ends(jax.random.randint(key_of[3], (QUERIES,), 0, CANDS), jax.random.fold_in(key_of[3], 1), 0, CANDS - 1).astype(jnp.int32)
    return dict(queries=queries, passages=passages, pair_block=pair_block, positives=positives)


def weigh(scores, picks):
    top = jnp.max(scores, axis=1, keepdims=True)
    shifted = jnp.exp(scores - top)
    total = jnp.sum(shifted, axis=1, keepdims=True)
    probs = shifted / total
    hits = picks[:, None] == lax.broadcasted_iota(jnp.int32, scores.shape, 1)
    chosen = jnp.sum(jnp.where(hits, scores, 0.0), axis=1)
    losses = top[:, 0] + jnp.log(total[:, 0]) - chosen
    weights = (probs - hits.astype(scores.dtype)).astype(jnp.bfloat16)
    return weights, jnp.sum(losses)


def reference(queries, passages, pair_block, positives):
    groups = jnp.arange(N_DP, dtype=jnp.int32)[None, :] * (PB_DEV * PBLK)
    starts = groups + pair_block.astype(jnp.int32) * PBLK
    inner = jnp.arange(PBLK, dtype=jnp.int32)[None, None, :]
    rows = (starts[:, :, None] + inner).reshape(N_DP, CANDS).astype(jnp.int32)

    def step(grads, inputs):
        block_q, index, picks = inputs
        cands = passages[index]
        scores = jnp.dot(block_q, cands.T, preferred_element_type=jnp.float32)
        weights, loss_sum = weigh(scores, picks)
        query_part = jnp.dot(weights, cands, preferred_element_type=jnp.float32)
        cand_grad = jnp.dot(weights.T, block_q, preferred_element_type=jnp.float32)
        grads = grads.at[index].add(cand_grad)
        return grads, (query_part, loss_sum)

    start = jnp.zeros((PASSAGES, D), jnp.float32)
    grads, (query_parts, loss_sums) = lax.scan(
        step, start,
        (queries.reshape(N_DP, QBLK, D), rows, positives.reshape(N_DP, QBLK)))
    loss = jnp.sum(loss_sums) / QUERIES
    return loss, query_parts.reshape(QUERIES, D), grads
```

```python
import jax
import jax.numpy as jnp
from jax import lax
from jax.experimental import pallas as pl
from jax.experimental.pallas import tpu as pltpu
from jax.sharding import Mesh, PartitionSpec as P

NZ, NY, NC, NX = 16, 4, 2, 4
NB = NY * NC
QBLK = 192
PBLK = 16
PB_DEV = 4
GROUP = PBLK * PB_DEV
QUERIES = NZ * NB * QBLK
CAND = NZ * PBLK
SHARE = QBLK // NX
DP = ("z", "y", "core")
ROW = ("y", "core", "x")


def pick_rows(sel_ref, p_ref, chosen, b):
    for z in range(NZ):
        start = pl.multiple_of(z * GROUP + sel_ref[z * NB + b] * PBLK, PBLK)
        chosen[z * PBLK : (z + 1) * PBLK, :] = p_ref[pl.ds(start, PBLK), :]


def scores_kernel(sel_ref, tab_ref, q_ref, p_ref, s_ref, chosen):
    pick_rows(sel_ref, p_ref, chosen, pl.program_id(0))
    s_ref[...] = lax.dot_general(
        q_ref[0], chosen[...], (((1,), (1,)), ((), ())), preferred_element_type=jnp.float32
    )


def partial_scores(sel, tab, q_all, p_all):
    width = q_all.shape[2]
    return pl.pallas_call(
        scores_kernel,
        out_shape=jax.ShapeDtypeStruct((NB * QBLK, CAND), jnp.float32),
        grid_spec=pltpu.PrefetchScalarGridSpec(
            num_scalar_prefetch=2,
            grid=(NB,),
            in_specs=[
                pl.BlockSpec((1, QBLK, width), lambda b, sel, tab: (tab[b], 0, 0)),
                pl.BlockSpec((NZ * GROUP, width), lambda b, sel, tab: (0, 0)),
            ],
            out_specs=pl.BlockSpec((QBLK, CAND), lambda b, sel, tab: (b, 0)),
            scratch_shapes=[pltpu.VMEM((CAND, width), jnp.bfloat16)],
        ),
        compiler_params=pltpu.CompilerParams(vmem_limit_bytes=40 << 20),
        cost_estimate=pl.CostEstimate(
            flops=2 * NB * QBLK * CAND * width,
            bytes_accessed=2 * (NB * QBLK + NZ * GROUP) * width + 4 * NB * QBLK * CAND,
            transcendentals=0,
        ),
        name="partial_scores",
    )(sel, tab, q_all, p_all)


def weigh_kernel(s_ref, pos_ref, w_ref, loss_ref, total):
    for j in range(NB):
        total[j] = (s_ref[j, 0] + s_ref[j, 1]) + (s_ref[j, 2] + s_ref[j, 3])
    scores = total[...]
    top = jnp.max(jnp.max(scores, axis=0), axis=1, keepdims=True)
    shifted = jnp.exp(scores - top[None])
    denom = jnp.sum(jnp.sum(shifted, axis=0), axis=1, keepdims=True)
    probs = shifted / denom[None]
    lane = lax.broadcasted_iota(jnp.int32, scores.shape, 2)
    col = lax.broadcasted_iota(jnp.int32, scores.shape, 0)
    index = ((lane // PBLK) * NB + col) * PBLK + lane % PBLK
    hits = index == pos_ref[...][None]
    chosen = jnp.sum(jnp.sum(jnp.where(hits, scores, 0.0), axis=0), axis=1, keepdims=True)
    weights = (probs - hits.astype(jnp.float32)).astype(jnp.bfloat16)
    for x in range(NX):
        w_ref[:, x] = weights
    loss = jnp.sum(top + jnp.log(denom) - chosen, axis=0, keepdims=True)
    loss_ref[...] = jnp.broadcast_to(loss, loss_ref.shape)


def weigh(parts, picks):
    return pl.pallas_call(
        weigh_kernel,
        out_shape=(
            jax.ShapeDtypeStruct((NB, NX, SHARE, CAND), jnp.bfloat16),
            jax.ShapeDtypeStruct((8, 128), jnp.float32),
        ),
        scratch_shapes=[pltpu.VMEM((NB, SHARE, CAND), jnp.float32)],
        compiler_params=pltpu.CompilerParams(vmem_limit_bytes=40 << 20),
        cost_estimate=pl.CostEstimate(
            flops=20 * NB * SHARE * CAND, bytes_accessed=6 * NB * NX * SHARE * CAND, transcendentals=NB * SHARE * CAND
        ),
        name="weigh",
    )(parts, picks)


def grads_kernel(sel_ref, tab_ref, out_ref, q_ref, p_ref, w_ref, qg_ref, pg_ref, chosen):
    b = pl.program_id(0)

    @pl.when(b == 0)
    def _():
        pg_ref[...] = jnp.zeros_like(pg_ref)

    pick_rows(sel_ref, p_ref, chosen, b)
    weights = w_ref[...]
    qg_ref[0] = jnp.dot(weights, chosen[...], preferred_element_type=jnp.float32)
    cand = lax.dot_general(
        weights, q_ref[0], (((0,), (0,)), ((), ())), preferred_element_type=jnp.float32
    )
    for z in range(NZ):
        start = pl.multiple_of(z * GROUP + sel_ref[z * NB + b] * PBLK, PBLK)
        pg_ref[pl.ds(start, PBLK), :] += cand[z * PBLK : (z + 1) * PBLK, :]


def grads(sel, tab, out, q_all, p_all, weights):
    width = q_all.shape[2]
    return pl.pallas_call(
        grads_kernel,
        out_shape=(
            jax.ShapeDtypeStruct((NB, QBLK, width), jnp.float32),
            jax.ShapeDtypeStruct((NZ * GROUP, width), jnp.float32),
        ),
        grid_spec=pltpu.PrefetchScalarGridSpec(
            num_scalar_prefetch=3,
            grid=(NB,),
            in_specs=[
                pl.BlockSpec((1, QBLK, width), lambda b, sel, tab, out: (tab[b], 0, 0)),
                pl.BlockSpec((NZ * GROUP, width), lambda b, sel, tab, out: (0, 0)),
                pl.BlockSpec((QBLK, CAND), lambda b, sel, tab, out: (b, 0)),
            ],
            out_specs=(
                pl.BlockSpec((1, QBLK, width), lambda b, sel, tab, out: (out[b], 0, 0)),
                pl.BlockSpec((NZ * GROUP, width), lambda b, sel, tab, out: (0, 0)),
            ),
            scratch_shapes=[pltpu.VMEM((CAND, width), jnp.bfloat16)],
        ),
        compiler_params=pltpu.CompilerParams(vmem_limit_bytes=40 << 20),
        cost_estimate=pl.CostEstimate(
            flops=4 * NB * QBLK * CAND * width,
            bytes_accessed=(6 * NB * QBLK + 6 * NZ * GROUP) * width + 2 * NB * QBLK * CAND,
            transcendentals=0,
        ),
        name="grads",
    )(sel, tab, out, q_all, p_all, weights)


def total_over(value, axis, size):
    copies = jnp.broadcast_to(value[None], (size,) + value.shape)
    return jnp.sum(lax.all_to_all(copies, axis, split_axis=0, concat_axis=0, tiled=True), axis=0)


def per_device(queries, passages, pair_block, positives):
    y, core, x = lax.axis_index("y"), lax.axis_index("core"), lax.axis_index("x")
    p_all = lax.all_gather(passages, "z", axis=0, tiled=True)
    sel = lax.all_to_all(
        pair_block.reshape(NZ, NB), "z", split_axis=0, concat_axis=0, tiled=True
    ).reshape(NZ * NB)
    parts = [queries]
    for k in range(1, NY):
        parts.append(lax.ppermute(queries, "y", [(i, (i + k) % NY) for i in range(NY)]))
    mine = jnp.stack(parts)
    other = lax.ppermute(mine, "core", [(0, 1), (1, 0)])
    q_all = jnp.concatenate([mine, other], axis=0)
    block = jnp.arange(NB, dtype=jnp.int32)
    block_y, away = block // NC, ((block % NC) != core).astype(jnp.int32)
    tab = away * NY + (y - block_y + NY) % NY
    out = away * NY + block_y

    part = partial_scores(sel, tab, q_all, p_all)
    swapped = lax.all_to_all(
        part.reshape(NB * NX, SHARE, CAND), ROW, split_axis=0, concat_axis=0, tiled=True
    )
    picks = lax.dynamic_slice(positives, (x * SHARE,), (SHARE,)).reshape(SHARE, 1)
    weights, loss = weigh(swapped.reshape(NB, NX, SHARE, CAND), picks)
    weights = lax.all_to_all(
        weights.reshape(NB * NX, SHARE, CAND), ROW, split_axis=0, concat_axis=0, tiled=True
    ).reshape(NB * QBLK, CAND)
    query_part, passage_part = grads(sel, tab, out, q_all, p_all, weights)

    passage_grad = lax.psum_scatter(passage_part, "z", scatter_dimension=0, tiled=True)
    arrived = lax.ppermute(query_part[NY:], "core", [(0, 1), (1, 0)])
    query_grad = jnp.sum(
        lax.all_to_all(query_part[:NY] + arrived, "y", split_axis=0, concat_axis=0, tiled=True),
        axis=0,
    )
    loss = total_over(total_over(loss, ROW, NB * NX), "z", NZ)[0, 0] / QUERIES
    return loss, query_grad, passage_grad


def solution(mesh):
    fine = Mesh(mesh.devices.reshape(NZ, NY, NC, NX), DP + ("x",))
    in_specs = (P(DP, "x"), P(DP, "x"), P(None, DP), P(DP))
    out_specs = (P(), P(DP, "x"), P(DP, "x"))
    return jax.shard_map(
        per_device, mesh=fine, in_specs=in_specs, out_specs=out_specs, check_vma=False
    )
```

```python
import jax
import jax.numpy as jnp
from jax import lax
from jax.experimental import pallas as pl
from jax.experimental.pallas import tpu as pltpu
from jax.sharding import Mesh, PartitionSpec as P

NZ, NY, NC, NX = 16, 4, 2, 4
NB = NY * NC
QBLK = 192
PBLK = 16
PB_DEV = 4
GROUP = PBLK * PB_DEV
QUERIES = NZ * NB * QBLK
CAND = NZ * PBLK
SHARE = NB * QBLK // NX
SENT = SHARE + 16
PER_X = NB // NX
LANES = 128
DP = ("z", "y", "core")
COL = ("y", "core")


def in_hbm(array):
    return pltpu.with_memory_space_constraint(array, pltpu.HBM)


def pick_rows(sel_ref, p_ref, chosen, b):
    for z in range(NZ):
        start = pl.multiple_of(z * GROUP + sel_ref[z, b] * PBLK, PBLK)
        chosen[z * PBLK : (z + 1) * PBLK, :] = p_ref[pl.ds(start, PBLK), :]


def encode_kernel(p_ref, pick_ref, q_ref, pos_ref, code_ref, out_ref):
    width = p_ref.shape[1]
    rows = p_ref[...].astype(jnp.float32)
    largest = jnp.maximum(jnp.max(jnp.abs(rows), axis=1, keepdims=True), 2.0**-126)
    shift = 13.0 - jnp.floor(jnp.log2(largest))
    half = jnp.floor(shift * 0.5)
    code_ref[:, :width] = rows * jnp.exp2(half) * jnp.exp2(shift - half)
    lane = lax.broadcasted_iota(jnp.int32, (GROUP, LANES), 1)
    spare = jnp.where(lane == LANES - 1, shift, 0.0)
    code_ref[:, width:] = spare
    picks = jnp.broadcast_to(pick_ref[...].astype(jnp.float32), (8, LANES))
    row = lax.broadcasted_iota(jnp.int32, (8, LANES), 0)
    picks = jnp.where(row == 0, picks, pltpu.roll(picks, LANES // 2, 1))
    code_ref[:8, width:] = jnp.where(lane[:8] < LANES // 2, picks, spare[:8])
    out_ref[:, :width] = q_ref[...]
    row = lax.broadcasted_iota(jnp.int32, (QBLK, QBLK), 0)
    col = lax.broadcasted_iota(jnp.int32, (QBLK, QBLK), 1)
    pos = jnp.where(row == col, pos_ref[...].astype(jnp.float32), 0.0)
    pos = jnp.sum(pos, axis=1, keepdims=True)
    high = jnp.floor(pos * (1.0 / LANES))
    lane = lax.broadcasted_iota(jnp.int32, (QBLK, LANES), 1)
    digits = jnp.where(lane == 0, high, jnp.where(lane == 1, pos - high * LANES, 0.0))
    out_ref[:, width:] = digits.astype(jnp.bfloat16)


def encode(passages, pair_block, queries, positives):
    rows, width = passages.shape
    scaled, marked = pl.pallas_call(
        encode_kernel,
        out_shape=(
            jax.ShapeDtypeStruct((rows, width + LANES), jnp.float32),
            jax.ShapeDtypeStruct((QBLK, width + LANES), jnp.bfloat16),
        ),
        compiler_params=pltpu.CompilerParams(vmem_limit_bytes=8 << 20),
        cost_estimate=pl.CostEstimate(
            flops=4 * rows * width, bytes_accessed=6 * rows * width, transcendentals=3 * rows
        ),
        name="encode",
    )(
        in_hbm(passages),
        in_hbm(pair_block.reshape(1, NZ * NB)),
        in_hbm(queries),
        in_hbm(positives.reshape(1, QBLK)),
    )
    return scaled.astype(jnp.float16), marked

def scores_kernel(at_ref, q_ref, c_ref, s_ref, p_ref, sel_ref, coded, held, passages, scores, chosen, picks, picked, sems):
    width = p_ref.shape[1]
    chunk = NZ * GROUP // NB

    def fetch_code(b):
        at = pl.ds(b * chunk, chunk)
        return pltpu.make_async_copy(c_ref.at[at], coded.at[at], sems.at[3, b])

    def fetch(b):
        return pltpu.make_async_copy(q_ref.at[b, :, pl.ds(0, width)], held.at[b], sems.at[0, b])

    def keep(b):
        at = pl.ds(b * chunk, chunk)
        return pltpu.make_async_copy(passages.at[at], p_ref.at[at], sems.at[1, b])

    def send(b):
        at = pl.ds(b * QBLK, QBLK)
        return pltpu.make_async_copy(scores.at[at], s_ref.at[at], sems.at[2, b])

    for b in range(NB):
        fetch_code(b).start()
    for b in range(NB):
        fetch(b).start()
    first = lax.rem(at_ref[0], LANES // 2)
    lower = at_ref[0] < LANES // 2
    for b in range(NB):
        fetch_code(b).wait()
        for z in range(b * chunk // GROUP, (b + 1) * chunk // GROUP):
            spare = coded[z * GROUP : z * GROUP + PBLK, width:].astype(jnp.int32)
            picks[z : z + 1, :] = jnp.where(lower, spare[:1], spare[1:2])
        at = pl.ds(b * chunk, chunk)
        code = coded[at]
        shift = code[:, width:][:, LANES - 1 :].astype(jnp.float32)
        half = jnp.floor(shift * 0.5)
        low, high = jnp.exp2(half - shift), jnp.exp2(-half)
        passages[at] = (code[:, :width].astype(jnp.float32) * low * high).astype(jnp.bfloat16)
        keep(b).start()
    picks[...] = pltpu.roll(picks[...], LANES - first, 1)
    local = pltpu.make_async_copy(picks, picked, sems.at[4, 0])
    local.start()
    local.wait()
    tell = pltpu.make_async_copy(picks, sel_ref, sems.at[4, 1])
    tell.start()
    for b in range(NB):
        pick_rows(picked, passages, chosen, b)
        fetch(b).wait()
        scores[pl.ds(b * QBLK, QBLK), :] = lax.dot_general(
            held[b], chosen[...], (((1,), (1,)), ((), ())), preferred_element_type=jnp.float32
        )
        send(b).start()
    tell.wait()
    for b in range(NB):
        keep(b).wait()
        send(b).wait()


def partial_scores(at, q_all, coded):
    width = q_all.shape[2] - LANES
    apart = pl.BlockSpec(memory_space=pl.ANY)
    return pl.pallas_call(
        scores_kernel,
        out_shape=(
            pltpu.HBM((NB * QBLK, CAND), jnp.float32),
            pltpu.HBM((NZ * GROUP, width), jnp.bfloat16),
            pltpu.HBM((NZ, LANES), jnp.int32),
        ),
        in_specs=[pl.BlockSpec(memory_space=pltpu.SMEM), apart, apart],
        out_specs=(apart, apart, apart),
        scratch_shapes=[
            pltpu.VMEM((NZ * GROUP, width + LANES), jnp.bfloat16),
            pltpu.VMEM((NB, QBLK, width), jnp.bfloat16),
            pltpu.VMEM((NZ * GROUP, width), jnp.bfloat16),
            pltpu.VMEM((NB * QBLK, CAND), jnp.float32),
            pltpu.VMEM((CAND, width), jnp.bfloat16),
            pltpu.VMEM((NZ, LANES), jnp.int32),
            pltpu.SMEM((NZ, LANES), jnp.int32),
            pltpu.SemaphoreType.DMA((5, NB)),
        ],
        compiler_params=pltpu.CompilerParams(vmem_limit_bytes=20 << 20),
        cost_estimate=pl.CostEstimate(
            flops=2 * NB * QBLK * CAND * width,
            bytes_accessed=2 * (NB * QBLK + 2 * NZ * GROUP) * width + 4 * NB * QBLK * CAND,
            transcendentals=0,
        ),
        name="partial_scores",
    )(at, in_hbm(q_all), in_hbm(coded))


def hits_of(digit_ref, col):
    digits = digit_ref[...].astype(jnp.float32)
    pos = (digits[:, :1] * LANES + digits[:, 1:2]).astype(jnp.int32)
    lane = lax.broadcasted_iota(jnp.int32, (SHARE, CAND), 1)
    return ((lane // PBLK) * NB + col) * PBLK + lane % PBLK == pos


def stats_kernel(col_ref, part_ref, digit_ref, s_ref, hit_ref, stat_ref):
    scores = (part_ref[0] + part_ref[1]) + (part_ref[2] + part_ref[3])
    s_ref[...] = scores
    top = jnp.max(scores, axis=1, keepdims=True)
    total = jnp.sum(jnp.exp(scores - top), axis=1, keepdims=True)
    hits = hits_of(digit_ref, col_ref[0])
    hit_ref[...] = hits.astype(jnp.float32)
    chosen = jnp.sum(jnp.where(hits, scores, 0.0), axis=1, keepdims=True)
    lane = lax.broadcasted_iota(jnp.int32, (SHARE, LANES), 1)
    packed = jnp.where(lane == 0, top, jnp.where(lane == 1, total, jnp.where(lane == 2, chosen, 0.0)))
    rows = packed.T[:8]
    for j in range(NB):
        stat_ref[j] = rows


def column_stats(col, parts, digits):
    return pl.pallas_call(
        stats_kernel,
        out_shape=(
            jax.ShapeDtypeStruct((SHARE, CAND), jnp.float32),
            jax.ShapeDtypeStruct((SHARE, CAND), jnp.float32),
            jax.ShapeDtypeStruct((NB, 8, SHARE), jnp.float32),
        ),
        in_specs=[
            pl.BlockSpec(memory_space=pltpu.SMEM),
            pl.BlockSpec(memory_space=pltpu.VMEM),
            pl.BlockSpec(memory_space=pltpu.VMEM),
        ],
        compiler_params=pltpu.CompilerParams(vmem_limit_bytes=8 << 20),
        cost_estimate=pl.CostEstimate(
            flops=12 * SHARE * CAND, bytes_accessed=20 * SHARE * CAND, transcendentals=SHARE * CAND
        ),
        name="column_stats",
    )(col, parts, in_hbm(digits))


def weigh_kernel(s_ref, hit_ref, stat_ref, w_ref):
    tops, totals, picked = stat_ref[:, 0, :], stat_ref[:, 1, :], stat_ref[:, 2, :]
    top = jnp.max(tops, axis=0, keepdims=True)
    total = jnp.sum(totals * jnp.exp(tops - top), axis=0, keepdims=True)
    losses = top + jnp.log(total) - jnp.sum(picked, axis=0, keepdims=True)
    row = lax.broadcasted_iota(jnp.int32, (LANES, SHARE), 0)
    turned = jnp.where(row == 0, top, jnp.where(row == 1, total, 0.0)).T
    probs = jnp.exp(s_ref[...] - turned[:, :1]) / turned[:, 1:2]
    w_ref[:SHARE] = (probs - hit_ref[...]).astype(jnp.bfloat16)
    loss = jnp.sum(losses, axis=1, keepdims=True)
    first = loss.astype(jnp.bfloat16).astype(jnp.float32)
    second = (loss - first).astype(jnp.bfloat16).astype(jnp.float32)
    row = lax.broadcasted_iota(jnp.int32, (SENT - SHARE, CAND), 0)
    pieces = jnp.where(row == 1, second, jnp.where(row == 2, loss - first - second, 0.0))
    w_ref[SHARE:] = jnp.where(row == 0, first, pieces).astype(jnp.bfloat16)


def weigh(scores, hits, stats):
    return pl.pallas_call(
        weigh_kernel,
        out_shape=jax.ShapeDtypeStruct((SENT, CAND), jnp.bfloat16),
        compiler_params=pltpu.CompilerParams(vmem_limit_bytes=8 << 20),
        cost_estimate=pl.CostEstimate(
            flops=10 * SHARE * CAND, bytes_accessed=6 * SHARE * CAND, transcendentals=SHARE * CAND
        ),
        name="weigh",
    )(scores, hits, stats)


def block_weights(w_ref, b):
    start = pl.multiple_of(lax.rem(b, PER_X) * QBLK, QBLK)
    return w_ref[lax.div(b, PER_X), pl.ds(start, QBLK), :]


def passage_kernel(sel_ref, q_ref, w_ref, pg_ref, kept_ref, acc, sems):
    width = acc.shape[1]
    keep = pltpu.make_async_copy(w_ref, kept_ref, sems.at[NZ])
    keep.start()
    acc[...] = jnp.zeros_like(acc)

    def add(b, done):
        cand = lax.dot_general(
            block_weights(w_ref, b),
            q_ref[b][:, :width],
            (((0,), (0,)), ((), ())),
            preferred_element_type=jnp.float32,
        )
        for z in range(NZ):
            start = pl.multiple_of(z * GROUP + sel_ref[z, b] * PBLK, PBLK)
            acc[pl.ds(start, PBLK), :] += cand[z * PBLK : (z + 1) * PBLK, :]
            done(z)

    def send(z):
        at = pl.ds(z * GROUP, GROUP)
        return pltpu.make_async_copy(acc.at[at], pg_ref.at[at], sems.at[z])

    lax.fori_loop(0, NB - 1, lambda b, carry: add(b, lambda z: None), None)
    add(jnp.int32(NB - 1), lambda z: send(z).start())
    for z in range(NZ):
        send(z).wait()
    keep.wait()


def passage_part(sel, q_all, weights):
    width = q_all.shape[2] - LANES
    whole = pl.BlockSpec(memory_space=pltpu.VMEM)
    apart = pl.BlockSpec(memory_space=pl.ANY)
    return pl.pallas_call(
        passage_kernel,
        out_shape=(
            pltpu.HBM((NZ * GROUP, width), jnp.float32),
            pltpu.HBM(weights.shape, weights.dtype),
        ),
        grid_spec=pltpu.PrefetchScalarGridSpec(
            num_scalar_prefetch=1,
            grid=(),
            in_specs=[whole, whole],
            out_specs=(apart, apart),
            scratch_shapes=[
                pltpu.VMEM((NZ * GROUP, width), jnp.float32),
                pltpu.SemaphoreType.DMA((NZ + 1,)),
            ],
        ),
        compiler_params=pltpu.CompilerParams(vmem_limit_bytes=16 << 20),
        cost_estimate=pl.CostEstimate(
            flops=2 * NB * QBLK * CAND * width,
            bytes_accessed=(2 * NB * QBLK + 4 * NZ * GROUP) * width + 2 * NB * QBLK * CAND,
            transcendentals=0,
        ),
        name="passage_part",
    )(sel, q_all, weights)


def query_kernel(sel_ref, tab_ref, p_ref, w_ref, *rest):
    *arrived, qg_ref, chosen = rest
    b = tab_ref[pl.program_id(0)]
    pick_rows(sel_ref, p_ref, chosen, b)
    share = jnp.dot(block_weights(w_ref, b), chosen[...], preferred_element_type=jnp.float32)
    qg_ref[0] = share + arrived[0][0] if arrived else share


def query_part(sel, tab, p_all, weights, *arrived):
    width = p_all.shape[1]
    block = pl.BlockSpec((1, QBLK, width), lambda k, sel, tab: (k, 0, 0))
    return pl.pallas_call(
        query_kernel,
        out_shape=jax.ShapeDtypeStruct((NY, QBLK, width), jnp.float32),
        grid_spec=pltpu.PrefetchScalarGridSpec(
            num_scalar_prefetch=2,
            grid=(NY,),
            in_specs=[
                pl.BlockSpec((NZ * GROUP, width), lambda k, sel, tab: (0, 0)),
                pl.BlockSpec((NX, SENT, CAND), lambda k, sel, tab: (0, 0, 0)),
            ]
            + [block] * len(arrived),
            out_specs=block,
            scratch_shapes=[pltpu.VMEM((CAND, width), jnp.bfloat16)],
        ),
        compiler_params=pltpu.CompilerParams(vmem_limit_bytes=16 << 20),
        cost_estimate=pl.CostEstimate(
            flops=2 * NY * QBLK * CAND * width,
            bytes_accessed=(4 * NY * QBLK + 2 * NZ * GROUP) * width + 2 * NB * QBLK * CAND,
            transcendentals=0,
        ),
        name="query_part",
    )(sel, tab, in_hbm(p_all), in_hbm(weights), *arrived)


def total_over(value, axis, size):
    copies = jnp.broadcast_to(value[None], (size,) + value.shape)
    return jnp.sum(lax.all_to_all(copies, axis, split_axis=0, concat_axis=0, tiled=True), axis=0)


def per_device(queries, passages, pair_block, positives):
    z, core, x = lax.axis_index("z"), lax.axis_index("core"), lax.axis_index("x")
    width = queries.shape[1]
    col = (lax.axis_index("y") * NC + core).astype(jnp.int32).reshape(1)
    code, marked = encode(passages, pair_block, queries, positives)
    q_all = lax.all_gather(marked, COL, axis=0, tiled=False)
    coded = lax.all_gather(code, "z", axis=0, tiled=True).astype(jnp.bfloat16)
    part, p_all, sel = partial_scores((z * NB).astype(jnp.int32).reshape(1), q_all, coded)
    digits = lax.dynamic_slice(q_all, (x * PER_X, 0, width), (PER_X, QBLK, LANES)).reshape(SHARE, LANES)
    parts = lax.all_to_all(
        part.reshape(NX, SHARE, CAND), "x", split_axis=0, concat_axis=0, tiled=True
    )
    scores, hits, stats = column_stats(col, parts, digits)
    stats = lax.all_to_all(stats, COL, split_axis=0, concat_axis=0, tiled=True)
    weights = lax.all_gather(weigh(scores, hits, stats), "x", axis=0, tiled=False)
    loss = jnp.sum(weights[:, SHARE : SHARE + 3, :1].astype(jnp.float32))

    passages_part, weights = passage_part(sel, q_all, weights)
    passage_grad = lax.psum_scatter(passages_part, "z", scatter_dimension=0, tiled=True)
    mine = jnp.arange(NY, dtype=jnp.int32) * NC + core
    away = jnp.arange(NY, dtype=jnp.int32) * NC + (1 - core)
    arrived = lax.ppermute(query_part(sel, away, p_all, weights), "core", [(0, 1), (1, 0)])
    query_grad = jnp.sum(
        lax.all_to_all(
            query_part(sel, mine, p_all, weights, arrived),
            "y",
            split_axis=0,
            concat_axis=0,
            tiled=True,
        ),
        axis=0,
    )
    loss = total_over(jnp.full((8, LANES), loss), "z", NZ)[0, 0] / QUERIES
    return loss, query_grad, passage_grad


def solution(mesh):
    fine = Mesh(mesh.devices.reshape(NZ, NY, NC, NX), DP + ("x",))
    in_specs = (P(DP, "x"), P(DP, "x"), P(None, DP), P(DP))
    out_specs = (P(), P(DP, "x"), P(DP, "x"))
    return jax.shard_map(
        per_device, mesh=fine, in_specs=in_specs, out_specs=out_specs, check_vma=False
    )
```

```python
import jax
import jax.numpy as jnp
from jax import lax
from jax.experimental import pallas as pl
from jax.experimental.pallas import tpu as pltpu
from jax.sharding import Mesh, PartitionSpec as P

NZ, NY, NC, NX = 16, 4, 2, 4
NB = NY * NC
QBLK = 192
PBLK = 16
PB_DEV = 4
GROUP = PBLK * PB_DEV
QUERIES = NZ * NB * QBLK
CAND = NZ * PBLK
SHARE = NB * QBLK // NX
SENT = SHARE + 16
PER_X = NB // NX
LANES = 128
DP = ("z", "y", "core")
COL = ("y", "core")


def in_hbm(array):
    return pltpu.with_memory_space_constraint(array, pltpu.HBM)


def pick_rows(sel_ref, p_ref, chosen, b):
    for z in range(NZ):
        start = pl.multiple_of(z * GROUP + sel_ref[z, b] * PBLK, PBLK)
        chosen[z * PBLK : (z + 1) * PBLK, :] = p_ref[pl.ds(start, PBLK), :]


def encode_kernel(p_ref, pick_ref, q_ref, pos_ref, code_ref, out_ref):
    width = p_ref.shape[1]
    rows = p_ref[...].astype(jnp.float32)
    largest = jnp.maximum(jnp.max(jnp.abs(rows), axis=1, keepdims=True), 2.0**-126)
    shift = 13.0 - jnp.floor(jnp.log2(largest))
    half = jnp.floor(shift * 0.5)
    code_ref[:, :width] = rows * jnp.exp2(half) * jnp.exp2(shift - half)
    lane = lax.broadcasted_iota(jnp.int32, (GROUP, LANES), 1)
    spare = jnp.where(lane == LANES - 1, shift, 0.0)
    code_ref[:, width:] = spare
    picks = jnp.broadcast_to(pick_ref[...].astype(jnp.float32), (8, LANES))
    row = lax.broadcasted_iota(jnp.int32, (8, LANES), 0)
    picks = jnp.where(row == 0, picks, pltpu.roll(picks, LANES // 2, 1))
    code_ref[:8, width:] = jnp.where(lane[:8] < LANES // 2, picks, spare[:8])
    out_ref[:, :width] = q_ref[...]
    row = lax.broadcasted_iota(jnp.int32, (QBLK, QBLK), 0)
    col = lax.broadcasted_iota(jnp.int32, (QBLK, QBLK), 1)
    pos = jnp.where(row == col, pos_ref[...].astype(jnp.float32), 0.0)
    pos = jnp.sum(pos, axis=1, keepdims=True)
    high = jnp.floor(pos * (1.0 / LANES))
    lane = lax.broadcasted_iota(jnp.int32, (QBLK, LANES), 1)
    digits = jnp.where(lane == 0, high, jnp.where(lane == 1, pos - high * LANES, 0.0))
    out_ref[:, width:] = digits.astype(jnp.bfloat16)


def encode(passages, pair_block, queries, positives):
    rows, width = passages.shape
    scaled, marked = pl.pallas_call(
        encode_kernel,
        out_shape=(
            jax.ShapeDtypeStruct((rows, width + LANES), jnp.float32),
            jax.ShapeDtypeStruct((QBLK, width + LANES), jnp.bfloat16),
        ),
        compiler_params=pltpu.CompilerParams(vmem_limit_bytes=8 << 20),
        cost_estimate=pl.CostEstimate(
            flops=4 * rows * width, bytes_accessed=6 * rows * width, transcendentals=3 * rows
        ),
        name="encode",
    )(
        in_hbm(passages),
        in_hbm(pair_block.reshape(1, NZ * NB)),
        in_hbm(queries),
        in_hbm(positives.reshape(1, QBLK)),
    )
    return scaled.astype(jnp.float16), marked

def scores_kernel(at_ref, q_ref, c_ref, s_ref, p_ref, sel_ref, coded, held, passages, chosen, spares, picks, picked, sems):
    width = p_ref.shape[1]
    chunk = NZ * GROUP // NB

    def fetch_code(b):
        at = pl.ds(b * chunk, chunk)
        return pltpu.make_async_copy(c_ref.at[at], coded.at[at], sems.at[2, b])

    def fetch(b):
        return pltpu.make_async_copy(q_ref.at[b, :, pl.ds(0, width)], held.at[b], sems.at[0, b])

    def keep(b):
        at = pl.ds(b * chunk, chunk)
        return pltpu.make_async_copy(passages.at[at], p_ref.at[at], sems.at[1, b])

    side = pltpu.make_async_copy(c_ref.at[:, pl.ds(width, LANES)], spares, sems.at[3, 2])
    side.start()
    for b in range(NB):
        fetch_code(b).start()
    for b in range(NB):
        fetch(b).start()
    first = lax.rem(at_ref[2], LANES // 2)
    lower = at_ref[2] < LANES // 2
    side.wait()
    for z in range(NZ):
        spare = spares[z * GROUP : z * GROUP + PBLK, :].astype(jnp.int32)
        picks[z : z + 1, :] = jnp.where(lower, spare[:1], spare[1:2])
    picks[...] = pltpu.roll(picks[...], LANES - first, 1)
    local = pltpu.make_async_copy(picks, picked, sems.at[3, 0])
    local.start()
    tell = pltpu.make_async_copy(picks, sel_ref, sems.at[3, 1])
    tell.start()
    for b in range(NB):
        fetch_code(b).wait()
        at = pl.ds(b * chunk, chunk)
        code = coded[at]
        shift = code[:, width:][:, LANES - 1 :].astype(jnp.float32)
        half = jnp.floor(shift * 0.5)
        low, high = jnp.exp2(half - shift), jnp.exp2(-half)
        passages[at] = (code[:, :width].astype(jnp.float32) * low * high).astype(jnp.bfloat16)
        keep(b).start()
    local.wait()

    def step(b, carry):
        pick_rows(picked, passages, chosen, b)
        fetch(b).wait()
        at = pl.ds(pl.multiple_of(b * QBLK, QBLK), QBLK)
        s_ref[at, :] = lax.dot_general(
            held[b], chosen[...], (((1,), (1,)), ((), ())), preferred_element_type=jnp.float32
        )
        return carry

    lax.fori_loop(0, NB, step, None)
    tell.wait()
    for b in range(NB):
        keep(b).wait()


def partial_scores(at, q_all, coded):
    width = q_all.shape[2] - LANES
    apart = pl.BlockSpec(memory_space=pl.ANY)
    return pl.pallas_call(
        scores_kernel,
        out_shape=(
            jax.ShapeDtypeStruct((NB * QBLK, CAND), jnp.float32),
            pltpu.HBM((NZ * GROUP, width), jnp.bfloat16),
            pltpu.HBM((NZ, LANES), jnp.int32),
        ),
        in_specs=[pl.BlockSpec(memory_space=pltpu.SMEM), apart, apart],
        out_specs=(pl.BlockSpec(memory_space=pltpu.VMEM), apart, apart),
        scratch_shapes=[
            pltpu.VMEM((NZ * GROUP, width + LANES), jnp.bfloat16),
            pltpu.VMEM((NB, QBLK, width), jnp.bfloat16),
            pltpu.VMEM((NZ * GROUP, width), jnp.bfloat16),
            pltpu.VMEM((CAND, width), jnp.bfloat16),
            pltpu.VMEM((NZ * GROUP, LANES), jnp.bfloat16),
            pltpu.VMEM((NZ, LANES), jnp.int32),
            pltpu.SMEM((NZ, LANES), jnp.int32),
            pltpu.SemaphoreType.DMA((4, NB)),
        ],
        compiler_params=pltpu.CompilerParams(vmem_limit_bytes=20 << 20),
        cost_estimate=pl.CostEstimate(
            flops=2 * NB * QBLK * CAND * width,
            bytes_accessed=2 * (NB * QBLK + 2 * NZ * GROUP) * width + 4 * NB * QBLK * CAND,
            transcendentals=0,
        ),
        name="partial_scores",
    )(at, in_hbm(q_all), in_hbm(coded))


def hits_of(digits, col):
    digits = digits.astype(jnp.float32)
    pos = (digits[:, :1] * LANES + digits[:, 1:2]).astype(jnp.int32)
    lane = lax.broadcasted_iota(jnp.int32, (SHARE, CAND), 1)
    return ((lane // PBLK) * NB + col) * PBLK + lane % PBLK == pos


def stats_kernel(at_ref, part_ref, q_ref, s_ref, hit_ref, stat_ref, digits, sem):
    width = q_ref.shape[2] - LANES
    mine = q_ref.at[pl.ds(at_ref[1] * PER_X, PER_X), :, pl.ds(width, LANES)]
    copy = pltpu.make_async_copy(mine, digits, sem)
    copy.start()
    scores = (part_ref[0] + part_ref[1]) + (part_ref[2] + part_ref[3])
    s_ref[...] = scores
    top = jnp.max(scores, axis=1, keepdims=True)
    total = jnp.sum(jnp.exp(scores - top), axis=1, keepdims=True)
    copy.wait()
    hits = hits_of(digits[...].reshape(SHARE, LANES), at_ref[0])
    hit_ref[...] = hits.astype(jnp.float32)
    chosen = jnp.sum(jnp.where(hits, scores, 0.0), axis=1, keepdims=True)
    lane = lax.broadcasted_iota(jnp.int32, (SHARE, LANES), 1)
    packed = jnp.where(lane == 0, top, jnp.where(lane == 1, total, jnp.where(lane == 2, chosen, 0.0)))
    rows = packed.T[:8]
    for j in range(NB):
        stat_ref[j] = rows


def column_stats(at, parts, q_all):
    return pl.pallas_call(
        stats_kernel,
        out_shape=(
            jax.ShapeDtypeStruct((SHARE, CAND), jnp.float32),
            jax.ShapeDtypeStruct((SHARE, CAND), jnp.float32),
            jax.ShapeDtypeStruct((NB, 8, SHARE), jnp.float32),
        ),
        in_specs=[
            pl.BlockSpec(memory_space=pltpu.SMEM),
            pl.BlockSpec(memory_space=pltpu.VMEM),
            pl.BlockSpec(memory_space=pl.ANY),
        ],
        scratch_shapes=[
            pltpu.VMEM((PER_X, QBLK, LANES), jnp.bfloat16),
            pltpu.SemaphoreType.DMA,
        ],
        compiler_params=pltpu.CompilerParams(vmem_limit_bytes=8 << 20),
        cost_estimate=pl.CostEstimate(
            flops=12 * SHARE * CAND, bytes_accessed=20 * SHARE * CAND, transcendentals=SHARE * CAND
        ),
        name="column_stats",
    )(at, parts, in_hbm(q_all))


def weigh_kernel(s_ref, hit_ref, stat_ref, w_ref):
    tops, totals, picked = stat_ref[:, 0, :], stat_ref[:, 1, :], stat_ref[:, 2, :]
    top = jnp.max(tops, axis=0, keepdims=True)
    total = jnp.sum(totals * jnp.exp(tops - top), axis=0, keepdims=True)
    losses = top + jnp.log(total) - jnp.sum(picked, axis=0, keepdims=True)
    row = lax.broadcasted_iota(jnp.int32, (LANES, SHARE), 0)
    turned = jnp.where(row == 0, top, jnp.where(row == 1, total, 0.0)).T
    probs = jnp.exp(s_ref[...] - turned[:, :1]) / turned[:, 1:2]
    w_ref[:SHARE] = (probs - hit_ref[...]).astype(jnp.bfloat16)
    loss = jnp.sum(losses, axis=1, keepdims=True)
    first = loss.astype(jnp.bfloat16).astype(jnp.float32)
    second = (loss - first).astype(jnp.bfloat16).astype(jnp.float32)
    row = lax.broadcasted_iota(jnp.int32, (SENT - SHARE, CAND), 0)
    pieces = jnp.where(row == 1, second, jnp.where(row == 2, loss - first - second, 0.0))
    w_ref[SHARE:] = jnp.where(row == 0, first, pieces).astype(jnp.bfloat16)


def weigh(scores, hits, stats):
    return pl.pallas_call(
        weigh_kernel,
        out_shape=jax.ShapeDtypeStruct((SENT, CAND), jnp.bfloat16),
        compiler_params=pltpu.CompilerParams(vmem_limit_bytes=8 << 20),
        cost_estimate=pl.CostEstimate(
            flops=10 * SHARE * CAND, bytes_accessed=6 * SHARE * CAND, transcendentals=SHARE * CAND
        ),
        name="weigh",
    )(scores, hits, stats)


def block_weights(w_ref, b):
    start = pl.multiple_of(lax.rem(b, PER_X) * QBLK, QBLK)
    return w_ref[lax.div(b, PER_X), pl.ds(start, QBLK), :]


def passage_kernel(sel_ref, q_ref, w_ref, pg_ref, kept_ref, acc, sems):
    width = acc.shape[1]
    keep = pltpu.make_async_copy(w_ref, kept_ref, sems.at[NZ])
    keep.start()
    acc[...] = jnp.zeros_like(acc)

    def add(b, part, done):
        rows = CAND // 2
        cand = lax.dot_general(
            block_weights(w_ref, b)[:, part * rows : (part + 1) * rows],
            q_ref[b][:, :width],
            (((0,), (0,)), ((), ())),
            preferred_element_type=jnp.float32,
        )
        for k in range(NZ // 2):
            z = part * (NZ // 2) + k
            start = pl.multiple_of(z * GROUP + sel_ref[z, b] * PBLK, PBLK)
            acc[pl.ds(start, PBLK), :] += cand[k * PBLK : (k + 1) * PBLK, :]
            done(z)

    def send(z):
        at = pl.ds(z * GROUP, GROUP)
        return pltpu.make_async_copy(acc.at[at], pg_ref.at[at], sems.at[z])

    for part in range(2):
        for b in range(NB - 1):
            add(jnp.int32(b), part, lambda z: None)
        add(jnp.int32(NB - 1), part, lambda z: send(z).start())
    for z in range(NZ):
        send(z).wait()
    keep.wait()


def passage_part(sel, q_all, weights):
    width = q_all.shape[2] - LANES
    whole = pl.BlockSpec(memory_space=pltpu.VMEM)
    apart = pl.BlockSpec(memory_space=pl.ANY)
    return pl.pallas_call(
        passage_kernel,
        out_shape=(
            pltpu.HBM((NZ * GROUP, width), jnp.float32),
            pltpu.HBM(weights.shape, weights.dtype),
        ),
        grid_spec=pltpu.PrefetchScalarGridSpec(
            num_scalar_prefetch=1,
            grid=(),
            in_specs=[whole, whole],
            out_specs=(apart, apart),
            scratch_shapes=[
                pltpu.VMEM((NZ * GROUP, width), jnp.float32),
                pltpu.SemaphoreType.DMA((NZ + 1,)),
            ],
        ),
        compiler_params=pltpu.CompilerParams(vmem_limit_bytes=16 << 20),
        cost_estimate=pl.CostEstimate(
            flops=2 * NB * QBLK * CAND * width,
            bytes_accessed=(2 * NB * QBLK + 4 * NZ * GROUP) * width + 2 * NB * QBLK * CAND,
            transcendentals=0,
        ),
        name="passage_part",
    )(sel, q_all, weights)


def query_kernel(sel_ref, tab_ref, p_ref, w_ref, *rest):
    *arrived, qg_ref, chosen = rest
    b = tab_ref[pl.program_id(0)]
    pick_rows(sel_ref, p_ref, chosen, b)
    share = jnp.dot(block_weights(w_ref, b), chosen[...], preferred_element_type=jnp.float32)
    qg_ref[0] = share + arrived[0][0] if arrived else share


def query_part(sel, tab, p_all, weights, *arrived):
    width = p_all.shape[1]
    block = pl.BlockSpec((1, QBLK, width), lambda k, sel, tab: (k, 0, 0))
    return pl.pallas_call(
        query_kernel,
        out_shape=jax.ShapeDtypeStruct((NY, QBLK, width), jnp.float32),
        grid_spec=pltpu.PrefetchScalarGridSpec(
            num_scalar_prefetch=2,
            grid=(NY,),
            in_specs=[
                pl.BlockSpec((NZ * GROUP, width), lambda k, sel, tab: (0, 0)),
                pl.BlockSpec((NX, SENT, CAND), lambda k, sel, tab: (0, 0, 0)),
            ]
            + [block] * len(arrived),
            out_specs=block,
            scratch_shapes=[pltpu.VMEM((CAND, width), jnp.bfloat16)],
        ),
        compiler_params=pltpu.CompilerParams(vmem_limit_bytes=16 << 20),
        cost_estimate=pl.CostEstimate(
            flops=2 * NY * QBLK * CAND * width,
            bytes_accessed=(4 * NY * QBLK + 2 * NZ * GROUP) * width + 2 * NB * QBLK * CAND,
            transcendentals=0,
        ),
        name="query_part",
    )(sel, tab, in_hbm(p_all), in_hbm(weights), *arrived)


def total_over(value, axis, size):
    copies = jnp.broadcast_to(value[None], (size,) + value.shape)
    return jnp.sum(lax.all_to_all(copies, axis, split_axis=0, concat_axis=0, tiled=True), axis=0)


def per_device(queries, passages, pair_block, positives):
    z, core, x = lax.axis_index("z"), lax.axis_index("core"), lax.axis_index("x")
    width = queries.shape[1]
    at = jnp.stack([lax.axis_index("y") * NC + core, x, z * NB]).astype(jnp.int32)
    code, marked = encode(passages, pair_block, queries, positives)
    q_all = lax.all_gather(marked, COL, axis=0, tiled=False)
    coded = lax.all_gather(code, "z", axis=0, tiled=True).astype(jnp.bfloat16)
    part, p_all, sel = partial_scores(at, q_all, coded)
    parts = lax.all_to_all(
        part.reshape(NX, SHARE, CAND), "x", split_axis=0, concat_axis=0, tiled=True
    )
    scores, hits, stats = column_stats(at, parts, q_all)
    stats = lax.all_to_all(stats, COL, split_axis=0, concat_axis=0, tiled=True)
    weights = lax.all_gather(weigh(scores, hits, stats), "x", axis=0, tiled=False)
    loss = jnp.sum(weights[:, SHARE : SHARE + 3, :1].astype(jnp.float32))

    passages_part, weights = passage_part(sel, q_all, weights)
    passage_grad = lax.psum_scatter(passages_part, "z", scatter_dimension=0, tiled=True)
    mine = jnp.arange(NY, dtype=jnp.int32) * NC + core
    away = jnp.arange(NY, dtype=jnp.int32) * NC + (1 - core)
    arrived = lax.ppermute(query_part(sel, away, p_all, weights), "core", [(0, 1), (1, 0)])
    query_grad = jnp.sum(
        lax.all_to_all(
            query_part(sel, mine, p_all, weights, arrived),
            "y",
            split_axis=0,
            concat_axis=0,
            tiled=True,
        ),
        axis=0,
    )
    loss = total_over(jnp.full((8, LANES), loss), "z", NZ)[0, 0] / QUERIES
    return loss, query_grad, passage_grad


def solution(mesh):
    fine = Mesh(mesh.devices.reshape(NZ, NY, NC, NX), DP + ("x",))
    in_specs = (P(DP, "x"), P(DP, "x"), P(None, DP), P(DP))
    out_specs = (P(), P(DP, "x"), P(DP, "x"))
    return jax.shard_map(
        per_device, mesh=fine, in_specs=in_specs, out_specs=out_specs, check_vma=False
    )
```

```python
import jax
import jax.numpy as jnp
from jax import lax
from jax.experimental import pallas as pl
from jax.experimental.pallas import tpu as pltpu
from jax.sharding import Mesh, PartitionSpec as P

NZ, NY, NC, NX = 16, 4, 2, 4
NB = NY * NC
QBLK = 192
PBLK = 16
PB_DEV = 4
GROUP = PBLK * PB_DEV
QUERIES = NZ * NB * QBLK
CAND = NZ * PBLK
SHARE = NB * QBLK // NX
SENT = SHARE + 16
PER_X = NB // NX
HALVES = 2
TILES = GROUP // PBLK
LANES = 128
DP = ("z", "y", "core")
COL = ("y", "core")


def in_hbm(array):
    return pltpu.with_memory_space_constraint(array, pltpu.HBM)


def pick_rows(sel_ref, p_ref, chosen, b):
    for z in range(NZ):
        start = pl.multiple_of(z * GROUP + sel_ref[z, b] * PBLK, PBLK)
        chosen[z * PBLK : (z + 1) * PBLK, :] = p_ref[pl.ds(start, PBLK), :]


def encode_kernel(p_ref, pick_ref, q_ref, pos_ref, code_ref, out_ref):
    width = p_ref.shape[1]
    rows = p_ref[...].astype(jnp.float32)
    largest = jnp.maximum(jnp.max(jnp.abs(rows), axis=1, keepdims=True), 2.0**-126)
    shift = 13.0 - jnp.floor(jnp.log2(largest))
    half = jnp.floor(shift * 0.5)
    scaled = rows * jnp.exp2(half) * jnp.exp2(shift - half)
    slabs = width // LANES * TILES
    for s in range(slabs):
        t, j = s // TILES, s % TILES
        code_ref[s] = scaled[j * PBLK : (j + 1) * PBLK, t * LANES : (t + 1) * LANES]
    picks = jnp.broadcast_to(pick_ref[...].astype(jnp.float32), (PBLK, LANES))
    row = lax.broadcasted_iota(jnp.int32, (PBLK, LANES), 0)
    lane = lax.broadcasted_iota(jnp.int32, (PBLK, LANES), 1)
    spare = jnp.where(row == 0, picks, pltpu.roll(picks, LANES // 2, 1))
    spare = jnp.where((row < 2) & (lane < LANES // 2), spare, 0.0)
    for j in range(TILES):
        spare = jnp.where(lane == LANES - TILES + j, shift[j * PBLK : (j + 1) * PBLK], spare)
    code_ref[slabs] = spare
    out_ref[:, :width] = q_ref[...]
    row = lax.broadcasted_iota(jnp.int32, (QBLK, QBLK), 0)
    col = lax.broadcasted_iota(jnp.int32, (QBLK, QBLK), 1)
    pos = jnp.where(row == col, pos_ref[...].astype(jnp.float32), 0.0)
    pos = jnp.sum(pos, axis=1, keepdims=True)
    high = jnp.floor(pos * (1.0 / LANES))
    lane = lax.broadcasted_iota(jnp.int32, (QBLK, LANES), 1)
    digits = jnp.where(lane == 0, high, jnp.where(lane == 1, pos - high * LANES, 0.0))
    out_ref[:, width:] = digits.astype(jnp.bfloat16)


def encode(passages, pair_block, queries, positives):
    rows, width = passages.shape
    scaled, marked = pl.pallas_call(
        encode_kernel,
        out_shape=(
            jax.ShapeDtypeStruct((width // LANES * TILES + 1, PBLK, LANES), jnp.float32),
            jax.ShapeDtypeStruct((QBLK, width + LANES), jnp.bfloat16),
        ),
        compiler_params=pltpu.CompilerParams(vmem_limit_bytes=8 << 20),
        cost_estimate=pl.CostEstimate(
            flops=4 * rows * width, bytes_accessed=6 * rows * width, transcendentals=3 * rows
        ),
        name="encode",
    )(
        in_hbm(passages),
        in_hbm(pair_block.reshape(1, NZ * NB)),
        in_hbm(queries),
        in_hbm(positives.reshape(1, QBLK)),
    )
    return scaled.astype(jnp.float16), marked

def scores_kernel(at_ref, q_ref, c_ref, s_ref, p_ref, sel_ref, coded, held, passages, chosen, spares, picks, picked, sems):
    width = p_ref.shape[1]
    chunk = NZ * GROUP // NB

    slabs = width // LANES * TILES

    def fetch_code(b):
        at = pl.ds(b * chunk // GROUP, chunk // GROUP)
        return pltpu.make_async_copy(c_ref.at[at], coded.at[at], sems.at[2, b])

    def fetch(b):
        return pltpu.make_async_copy(q_ref.at[b, :, pl.ds(0, width)], held.at[b], sems.at[0, b])

    def keep(b):
        at = pl.ds(b * chunk, chunk)
        return pltpu.make_async_copy(passages.at[at], p_ref.at[at], sems.at[1, b])

    side = pltpu.make_async_copy(c_ref.at[:, slabs], spares, sems.at[3, 2])
    side.start()
    for b in range(NB):
        fetch_code(b).start()
    for b in range(NB):
        fetch(b).start()
    first = lax.rem(at_ref[2], LANES // 2)
    lower = at_ref[2] < LANES // 2
    side.wait()
    for z in range(NZ):
        spare = spares[z].astype(jnp.int32)
        picks[z : z + 1, :] = jnp.where(lower, spare[:1], spare[1:2])
    picks[...] = pltpu.roll(picks[...], LANES - first, 1)
    local = pltpu.make_async_copy(picks, picked, sems.at[3, 0])
    local.start()
    tell = pltpu.make_async_copy(picks, sel_ref, sems.at[3, 1])
    tell.start()
    for b in range(NB):
        fetch_code(b).wait()
        for z in range(b * chunk // GROUP, (b + 1) * chunk // GROUP):
            spare = spares[z].astype(jnp.float32)
            columns = [spare[:, LANES - TILES + j :][:, :1] for j in range(TILES)]
            shift = jnp.concatenate(columns, axis=0)
            half = jnp.floor(shift * 0.5)
            low, high = jnp.exp2(half - shift), jnp.exp2(-half)
            for t in range(width // LANES):
                value = coded[z, t * TILES : (t + 1) * TILES].astype(jnp.float32)
                value = value.reshape(GROUP, LANES) * low * high
                passages[z * GROUP : (z + 1) * GROUP, t * LANES : (t + 1) * LANES] = value.astype(
                    jnp.bfloat16
                )
        keep(b).start()
    local.wait()

    def step(b, carry):
        pick_rows(picked, passages, chosen, b)
        fetch(b).wait()
        at = pl.ds(pl.multiple_of(b * QBLK, QBLK), QBLK)
        s_ref[at, :] = lax.dot_general(
            held[b], chosen[...], (((1,), (1,)), ((), ())), preferred_element_type=jnp.float32
        )
        return carry

    lax.fori_loop(0, NB, step, None)
    tell.wait()
    for b in range(NB):
        keep(b).wait()


def partial_scores(at, q_all, coded):
    width = q_all.shape[2] - LANES
    apart = pl.BlockSpec(memory_space=pl.ANY)
    return pl.pallas_call(
        scores_kernel,
        out_shape=(
            jax.ShapeDtypeStruct((NB * QBLK, CAND), jnp.float32),
            pltpu.HBM((NZ * GROUP, width), jnp.bfloat16),
            pltpu.HBM((NZ, LANES), jnp.int32),
        ),
        in_specs=[pl.BlockSpec(memory_space=pltpu.SMEM), apart, apart],
        out_specs=(pl.BlockSpec(memory_space=pltpu.VMEM), apart, apart),
        scratch_shapes=[
            pltpu.VMEM((NZ, width // LANES * TILES + 1, PBLK, LANES), jnp.bfloat16),
            pltpu.VMEM((NB, QBLK, width), jnp.bfloat16),
            pltpu.VMEM((NZ * GROUP, width), jnp.bfloat16),
            pltpu.VMEM((CAND, width), jnp.bfloat16),
            pltpu.VMEM((NZ, PBLK, LANES), jnp.bfloat16),
            pltpu.VMEM((NZ, LANES), jnp.int32),
            pltpu.SMEM((NZ, LANES), jnp.int32),
            pltpu.SemaphoreType.DMA((4, NB)),
        ],
        compiler_params=pltpu.CompilerParams(vmem_limit_bytes=20 << 20),
        cost_estimate=pl.CostEstimate(
            flops=2 * NB * QBLK * CAND * width,
            bytes_accessed=2 * (NB * QBLK + 2 * NZ * GROUP) * width + 4 * NB * QBLK * CAND,
            transcendentals=0,
        ),
        name="partial_scores",
    )(at, in_hbm(q_all), in_hbm(coded))


def hits_of(digits, col):
    digits = digits.astype(jnp.float32)
    pos = (digits[:, :1] * LANES + digits[:, 1:2]).astype(jnp.int32)
    lane = lax.broadcasted_iota(jnp.int32, (SHARE, CAND), 1)
    return ((lane // PBLK) * NB + col) * PBLK + lane % PBLK == pos


def stats_kernel(at_ref, part_ref, q_ref, s_ref, hit_ref, stat_ref, digits, sem):
    width = q_ref.shape[2] - LANES
    mine = q_ref.at[pl.ds(at_ref[1] * PER_X, PER_X), :, pl.ds(width, LANES)]
    copy = pltpu.make_async_copy(mine, digits, sem)
    copy.start()
    scores = (part_ref[0] + part_ref[1]) + (part_ref[2] + part_ref[3])
    s_ref[...] = scores
    top = jnp.max(scores, axis=1, keepdims=True)
    total = jnp.sum(jnp.exp(scores - top), axis=1, keepdims=True)
    copy.wait()
    hits = hits_of(digits[...].reshape(SHARE, LANES), at_ref[0])
    hit_ref[...] = hits.astype(jnp.float32)
    chosen = jnp.sum(jnp.where(hits, scores, 0.0), axis=1, keepdims=True)
    lane = lax.broadcasted_iota(jnp.int32, (SHARE, LANES), 1)
    packed = jnp.where(lane == 0, top, jnp.where(lane == 1, total, jnp.where(lane == 2, chosen, 0.0)))
    rows = packed.T[:8]
    for j in range(NB):
        stat_ref[j] = rows


def column_stats(at, parts, q_all):
    return pl.pallas_call(
        stats_kernel,
        out_shape=(
            jax.ShapeDtypeStruct((SHARE, CAND), jnp.float32),
            jax.ShapeDtypeStruct((SHARE, CAND), jnp.float32),
            jax.ShapeDtypeStruct((NB, 8, SHARE), jnp.float32),
        ),
        in_specs=[
            pl.BlockSpec(memory_space=pltpu.SMEM),
            pl.BlockSpec(memory_space=pltpu.VMEM),
            pl.BlockSpec(memory_space=pl.ANY),
        ],
        scratch_shapes=[
            pltpu.VMEM((PER_X, QBLK, LANES), jnp.bfloat16),
            pltpu.SemaphoreType.DMA,
        ],
        compiler_params=pltpu.CompilerParams(vmem_limit_bytes=8 << 20),
        cost_estimate=pl.CostEstimate(
            flops=12 * SHARE * CAND, bytes_accessed=20 * SHARE * CAND, transcendentals=SHARE * CAND
        ),
        name="column_stats",
    )(at, parts, in_hbm(q_all))


def weigh_kernel(s_ref, hit_ref, stat_ref, w_ref):
    tops, totals, picked = stat_ref[:, 0, :], stat_ref[:, 1, :], stat_ref[:, 2, :]
    top = jnp.max(tops, axis=0, keepdims=True)
    total = jnp.sum(totals * jnp.exp(tops - top), axis=0, keepdims=True)
    losses = top + jnp.log(total) - jnp.sum(picked, axis=0, keepdims=True)
    row = lax.broadcasted_iota(jnp.int32, (LANES, SHARE), 0)
    turned = jnp.where(row == 0, top, jnp.where(row == 1, total, 0.0)).T
    probs = jnp.exp(s_ref[...] - turned[:, :1]) / turned[:, 1:2]
    weights = (probs - hit_ref[...]).astype(jnp.bfloat16)
    loss = jnp.sum(losses, axis=1, keepdims=True)
    first = loss.astype(jnp.bfloat16).astype(jnp.float32)
    second = (loss - first).astype(jnp.bfloat16).astype(jnp.float32)
    row = lax.broadcasted_iota(jnp.int32, (SENT - SHARE, LANES), 0)
    pieces = jnp.where(row == 1, second, jnp.where(row == 2, loss - first - second, 0.0))
    pieces = jnp.where(row == 0, first, pieces).astype(jnp.bfloat16)
    for h in range(HALVES):
        w_ref[h, :SHARE] = weights[:, h * LANES : (h + 1) * LANES]
        w_ref[h, SHARE:] = pieces


def weigh(scores, hits, stats):
    return pl.pallas_call(
        weigh_kernel,
        out_shape=jax.ShapeDtypeStruct((HALVES, SENT, LANES), jnp.bfloat16),
        compiler_params=pltpu.CompilerParams(vmem_limit_bytes=8 << 20),
        cost_estimate=pl.CostEstimate(
            flops=10 * SHARE * CAND, bytes_accessed=6 * SHARE * CAND, transcendentals=SHARE * CAND
        ),
        name="weigh",
    )(scores, hits, stats)


def block_weights(w_ref, b):
    start = pl.multiple_of(lax.rem(b, PER_X) * QBLK, QBLK)
    slab = lax.div(b, PER_X) * HALVES
    return jnp.concatenate([w_ref[slab + h, pl.ds(start, QBLK), :] for h in range(HALVES)], axis=1)


def passage_kernel(sel_ref, q_ref, w_ref, pg_ref, kept_ref, acc, sems):
    width = acc.shape[1]
    keep = pltpu.make_async_copy(w_ref, kept_ref, sems.at[NZ])
    keep.start()
    acc[...] = jnp.zeros_like(acc)

    def add(b, part, done):
        cand = lax.dot_general(
            w_ref[b // PER_X * HALVES + part, b % PER_X * QBLK : (b % PER_X + 1) * QBLK],
            q_ref[b][:, :width],
            (((0,), (0,)), ((), ())),
            preferred_element_type=jnp.float32,
        )
        for k in range(NZ // 2):
            z = part * (NZ // 2) + k
            start = pl.multiple_of(z * GROUP + sel_ref[z, b] * PBLK, PBLK)
            acc[pl.ds(start, PBLK), :] += cand[k * PBLK : (k + 1) * PBLK, :]
            done(z)

    def send(z):
        at = pl.ds(z * GROUP, GROUP)
        return pltpu.make_async_copy(acc.at[at], pg_ref.at[at], sems.at[z])

    for part in range(2):
        for b in range(NB - 1):
            add(b, part, lambda z: None)
        add(NB - 1, part, lambda z: send(z).start())
    for z in range(NZ):
        send(z).wait()
    keep.wait()


def passage_part(sel, q_all, weights):
    width = q_all.shape[2] - LANES
    whole = pl.BlockSpec(memory_space=pltpu.VMEM)
    apart = pl.BlockSpec(memory_space=pl.ANY)
    return pl.pallas_call(
        passage_kernel,
        out_shape=(
            pltpu.HBM((NZ * GROUP, width), jnp.float32),
            pltpu.HBM(weights.shape, weights.dtype),
        ),
        grid_spec=pltpu.PrefetchScalarGridSpec(
            num_scalar_prefetch=1,
            grid=(),
            in_specs=[whole, whole],
            out_specs=(apart, apart),
            scratch_shapes=[
                pltpu.VMEM((NZ * GROUP, width), jnp.float32),
                pltpu.SemaphoreType.DMA((NZ + 1,)),
            ],
        ),
        compiler_params=pltpu.CompilerParams(vmem_limit_bytes=16 << 20),
        cost_estimate=pl.CostEstimate(
            flops=2 * NB * QBLK * CAND * width,
            bytes_accessed=(2 * NB * QBLK + 4 * NZ * GROUP) * width + 2 * NB * QBLK * CAND,
            transcendentals=0,
        ),
        name="passage_part",
    )(sel, q_all, weights)


def query_kernel(sel_ref, tab_ref, p_ref, w_ref, *rest):
    *arrived, qg_ref, chosen = rest
    b = tab_ref[pl.program_id(0)]
    pick_rows(sel_ref, p_ref, chosen, b)
    share = jnp.dot(block_weights(w_ref, b), chosen[...], preferred_element_type=jnp.float32)
    qg_ref[0] = share + arrived[0][0] if arrived else share


def query_part(sel, tab, p_all, weights, *arrived):
    width = p_all.shape[1]
    block = pl.BlockSpec((1, QBLK, width), lambda k, sel, tab: (k, 0, 0))
    return pl.pallas_call(
        query_kernel,
        out_shape=jax.ShapeDtypeStruct((NY, QBLK, width), jnp.float32),
        grid_spec=pltpu.PrefetchScalarGridSpec(
            num_scalar_prefetch=2,
            grid=(NY,),
            in_specs=[
                pl.BlockSpec((NZ * GROUP, width), lambda k, sel, tab: (0, 0)),
                pl.BlockSpec((NX * HALVES, SENT, LANES), lambda k, sel, tab: (0, 0, 0)),
            ]
            + [block] * len(arrived),
            out_specs=block,
            scratch_shapes=[pltpu.VMEM((CAND, width), jnp.bfloat16)],
        ),
        compiler_params=pltpu.CompilerParams(vmem_limit_bytes=16 << 20),
        cost_estimate=pl.CostEstimate(
            flops=2 * NY * QBLK * CAND * width,
            bytes_accessed=(4 * NY * QBLK + 2 * NZ * GROUP) * width + 2 * NB * QBLK * CAND,
            transcendentals=0,
        ),
        name="query_part",
    )(sel, tab, in_hbm(p_all), in_hbm(weights), *arrived)


def total_over(value, axis, size):
    copies = jnp.broadcast_to(value[None], (size,) + value.shape)
    return jnp.sum(lax.all_to_all(copies, axis, split_axis=0, concat_axis=0, tiled=True), axis=0)


def per_device(queries, passages, pair_block, positives):
    z, core, x = lax.axis_index("z"), lax.axis_index("core"), lax.axis_index("x")
    width = queries.shape[1]
    at = jnp.stack([lax.axis_index("y") * NC + core, x, z * NB]).astype(jnp.int32)
    code, marked = encode(passages, pair_block, queries, positives)
    q_all = lax.all_gather(marked, COL, axis=0, tiled=False)
    coded = lax.all_gather(code, "z", axis=0, tiled=True).astype(jnp.bfloat16)
    coded = coded.reshape(NZ, *code.shape)
    part, p_all, sel = partial_scores(at, q_all, coded)
    parts = lax.all_to_all(
        part.reshape(NX, SHARE, CAND), "x", split_axis=0, concat_axis=0, tiled=True
    )
    scores, hits, stats = column_stats(at, parts, q_all)
    stats = lax.all_to_all(stats, COL, split_axis=0, concat_axis=0, tiled=True)
    weights = lax.all_gather(weigh(scores, hits, stats), "x", axis=0, tiled=True)
    loss = jnp.sum(weights[::HALVES, SHARE : SHARE + 3, :1].astype(jnp.float32))

    passages_part, weights = passage_part(sel, q_all, weights)
    passage_grad = lax.psum_scatter(passages_part, "z", scatter_dimension=0, tiled=True)
    mine = jnp.arange(NY, dtype=jnp.int32) * NC + core
    away = jnp.arange(NY, dtype=jnp.int32) * NC + (1 - core)
    arrived = lax.ppermute(query_part(sel, away, p_all, weights), "core", [(0, 1), (1, 0)])
    query_grad = jnp.sum(
        lax.all_to_all(
            query_part(sel, mine, p_all, weights, arrived),
            "y",
            split_axis=0,
            concat_axis=0,
            tiled=True,
        ),
        axis=0,
    )
    loss = total_over(jnp.full((8, LANES), loss), "z", NZ)[0, 0] / QUERIES
    return loss, query_grad, passage_grad


def solution(mesh):
    fine = Mesh(mesh.devices.reshape(NZ, NY, NC, NX), DP + ("x",))
    in_specs = (P(DP, "x"), P(DP, "x"), P(None, DP), P(DP))
    out_specs = (P(), P(DP, "x"), P(DP, "x"))
    return jax.shard_map(
        per_device, mesh=fine, in_specs=in_specs, out_specs=out_specs, check_vma=False
    )
```

```python
import jax
import jax.numpy as jnp
from jax import lax
from jax.experimental import pallas as pl
from jax.experimental.pallas import tpu as pltpu
from jax.sharding import Mesh, PartitionSpec as P

NZ, NY, NC, NX = 16, 4, 2, 4
NB = NY * NC
QBLK = 192
PBLK = 16
PB_DEV = 4
GROUP = PBLK * PB_DEV
QUERIES = NZ * NB * QBLK
CAND = NZ * PBLK
SHARE = NB * QBLK // NX
SENT = SHARE + 16
PER_X = NB // NX
HALVES = 2
TILES = GROUP // PBLK
LANES = 128
DP = ("z", "y", "core")
COL = ("y", "core")


def in_hbm(array):
    return pltpu.with_memory_space_constraint(array, pltpu.HBM)


def pick_rows(sel_ref, p_ref, chosen, b):
    for z in range(NZ):
        start = pl.multiple_of(z * GROUP + sel_ref[z, b] * PBLK, PBLK)
        chosen[z * PBLK : (z + 1) * PBLK, :] = p_ref[pl.ds(start, PBLK), :]


def encode_kernel(p_ref, pick_ref, q_ref, pos_ref, code_ref, out_ref):
    width = p_ref.shape[1]
    rows = p_ref[...].astype(jnp.float32)
    largest = jnp.maximum(jnp.max(jnp.abs(rows), axis=1, keepdims=True), 2.0**-126)
    shift = 13.0 - jnp.floor(jnp.log2(largest))
    half = jnp.floor(shift * 0.5)
    scaled = rows * jnp.exp2(half) * jnp.exp2(shift - half)
    slabs = width // LANES * TILES
    for s in range(slabs):
        t, j = s // TILES, s % TILES
        code_ref[s] = scaled[j * PBLK : (j + 1) * PBLK, t * LANES : (t + 1) * LANES]
    picks = jnp.broadcast_to(pick_ref[...].astype(jnp.float32), (PBLK, LANES))
    row = lax.broadcasted_iota(jnp.int32, (PBLK, LANES), 0)
    lane = lax.broadcasted_iota(jnp.int32, (PBLK, LANES), 1)
    spare = jnp.where(row == 0, picks, pltpu.roll(picks, LANES // 2, 1))
    spare = jnp.where((row < 2) & (lane < LANES // 2), spare, 0.0)
    for j in range(TILES):
        spare = jnp.where(lane == LANES - TILES + j, shift[j * PBLK : (j + 1) * PBLK], spare)
    code_ref[slabs] = spare
    out_ref[:, :width] = q_ref[...]
    row = lax.broadcasted_iota(jnp.int32, (QBLK, QBLK), 0)
    col = lax.broadcasted_iota(jnp.int32, (QBLK, QBLK), 1)
    pos = jnp.where(row == col, pos_ref[...].astype(jnp.float32), 0.0)
    pos = jnp.sum(pos, axis=1, keepdims=True)
    high = jnp.floor(pos * (1.0 / LANES))
    lane = lax.broadcasted_iota(jnp.int32, (QBLK, LANES), 1)
    digits = jnp.where(lane == 0, high, jnp.where(lane == 1, pos - high * LANES, 0.0))
    out_ref[:, width:] = digits.astype(jnp.bfloat16)


def encode(passages, pair_block, queries, positives):
    rows, width = passages.shape
    scaled, marked = pl.pallas_call(
        encode_kernel,
        out_shape=(
            jax.ShapeDtypeStruct((width // LANES * TILES + 1, PBLK, LANES), jnp.float32),
            jax.ShapeDtypeStruct((QBLK, width + LANES), jnp.bfloat16),
        ),
        compiler_params=pltpu.CompilerParams(vmem_limit_bytes=8 << 20),
        cost_estimate=pl.CostEstimate(
            flops=4 * rows * width, bytes_accessed=6 * rows * width, transcendentals=3 * rows
        ),
        name="encode",
    )(
        in_hbm(passages),
        in_hbm(pair_block.reshape(1, NZ * NB)),
        in_hbm(queries),
        in_hbm(positives.reshape(1, QBLK)),
    )
    return scaled.astype(jnp.float16), marked

def scores_kernel(at_ref, q_ref, c_ref, s_ref, p_ref, sel_ref, coded, held, passages, chosen, spares, picks, picked, sems):
    width = p_ref.shape[1]
    chunk = NZ * GROUP // NB

    slabs = width // LANES * TILES

    def exponents(tile):
        return jnp.concatenate([tile[:, LANES - TILES + j :][:, :1] for j in range(TILES)], axis=0)

    def fetch_code(b):
        at = pl.ds(b * chunk // GROUP, chunk // GROUP)
        return pltpu.make_async_copy(c_ref.at[at], coded.at[at], sems.at[2, b])

    def fetch(b):
        return pltpu.make_async_copy(q_ref.at[b, :, pl.ds(0, width)], held.at[b], sems.at[0, b])

    def keep(b):
        at = pl.ds(b * chunk, chunk)
        return pltpu.make_async_copy(passages.at[at], p_ref.at[at], sems.at[1, b])

    side = pltpu.make_async_copy(c_ref.at[:, slabs], spares, sems.at[3, 2])
    side.start()
    for b in range(NB):
        fetch_code(b).start()
    for b in range(NB):
        fetch(b).start()
    first = lax.rem(at_ref[2], LANES // 2)
    lower = at_ref[2] < LANES // 2
    side.wait()
    for z in range(NZ):
        spare = spares[z].astype(jnp.int32)
        picks[z : z + 1, :] = jnp.where(lower, spare[:1], spare[1:2])
    picks[...] = pltpu.roll(picks[...], LANES - first, 1)
    local = pltpu.make_async_copy(picks, picked, sems.at[3, 0])
    local.start()
    tell = pltpu.make_async_copy(picks, sel_ref, sems.at[3, 1])
    tell.start()
    for b in range(NB):
        fetch_code(b).wait()
        for z in range(b * chunk // GROUP, (b + 1) * chunk // GROUP):
            shift = spares[z].astype(jnp.float32)
            half = jnp.floor(shift * 0.5)
            low, high = exponents(jnp.exp2(half - shift)), exponents(jnp.exp2(-half))
            for t in range(width // LANES):
                value = coded[z, t * TILES : (t + 1) * TILES].astype(jnp.float32)
                value = value.reshape(GROUP, LANES) * low * high
                passages[z * GROUP : (z + 1) * GROUP, t * LANES : (t + 1) * LANES] = value.astype(
                    jnp.bfloat16
                )
        keep(b).start()
    local.wait()

    def step(b, carry):
        pick_rows(picked, passages, chosen, b)
        fetch(b).wait()
        at = pl.ds(pl.multiple_of(b * QBLK, QBLK), QBLK)
        s_ref[at, :] = lax.dot_general(
            held[b], chosen[...], (((1,), (1,)), ((), ())), preferred_element_type=jnp.float32
        )
        return carry

    lax.fori_loop(0, NB, step, None)
    tell.wait()
    for b in range(NB):
        keep(b).wait()


def partial_scores(at, q_all, coded):
    width = q_all.shape[2] - LANES
    apart = pl.BlockSpec(memory_space=pl.ANY)
    return pl.pallas_call(
        scores_kernel,
        out_shape=(
            jax.ShapeDtypeStruct((NB * QBLK, CAND), jnp.float32),
            pltpu.HBM((NZ * GROUP, width), jnp.bfloat16),
            pltpu.HBM((NZ, LANES), jnp.int32),
        ),
        in_specs=[pl.BlockSpec(memory_space=pltpu.SMEM), apart, apart],
        out_specs=(pl.BlockSpec(memory_space=pltpu.VMEM), apart, apart),
        scratch_shapes=[
            pltpu.VMEM((NZ, width // LANES * TILES + 1, PBLK, LANES), jnp.bfloat16),
            pltpu.VMEM((NB, QBLK, width), jnp.bfloat16),
            pltpu.VMEM((NZ * GROUP, width), jnp.bfloat16),
            pltpu.VMEM((CAND, width), jnp.bfloat16),
            pltpu.VMEM((NZ, PBLK, LANES), jnp.bfloat16),
            pltpu.VMEM((NZ, LANES), jnp.int32),
            pltpu.SMEM((NZ, LANES), jnp.int32),
            pltpu.SemaphoreType.DMA((4, NB)),
        ],
        compiler_params=pltpu.CompilerParams(vmem_limit_bytes=20 << 20),
        cost_estimate=pl.CostEstimate(
            flops=2 * NB * QBLK * CAND * width,
            bytes_accessed=2 * (NB * QBLK + 2 * NZ * GROUP) * width + 4 * NB * QBLK * CAND,
            transcendentals=0,
        ),
        name="partial_scores",
    )(at, in_hbm(q_all), in_hbm(coded))


def hits_of(digits, col):
    digits = digits.astype(jnp.float32)
    pos = (digits[:, :1] * LANES + digits[:, 1:2]).astype(jnp.int32)
    lane = lax.broadcasted_iota(jnp.int32, (SHARE, CAND), 1)
    return ((lane // PBLK) * NB + col) * PBLK + lane % PBLK == pos


def stats_kernel(at_ref, part_ref, q_ref, s_ref, hit_ref, stat_ref, digits, sem):
    width = q_ref.shape[2] - LANES
    mine = q_ref.at[pl.ds(at_ref[1] * PER_X, PER_X), :, pl.ds(width, LANES)]
    copy = pltpu.make_async_copy(mine, digits, sem)
    copy.start()
    scores = (part_ref[0] + part_ref[1]) + (part_ref[2] + part_ref[3])
    s_ref[...] = scores
    top = jnp.max(scores, axis=1, keepdims=True)
    total = jnp.sum(jnp.exp(scores - top), axis=1, keepdims=True)
    copy.wait()
    hits = hits_of(digits[...].reshape(SHARE, LANES), at_ref[0])
    hit_ref[...] = hits.astype(jnp.float32)
    chosen = jnp.sum(jnp.where(hits, scores, 0.0), axis=1, keepdims=True)
    lane = lax.broadcasted_iota(jnp.int32, (SHARE, LANES), 1)
    packed = jnp.where(lane == 0, top, jnp.where(lane == 1, total, jnp.where(lane == 2, chosen, 0.0)))
    rows = packed.T[:8]
    for j in range(NB):
        stat_ref[j] = rows


def column_stats(at, parts, q_all):
    return pl.pallas_call(
        stats_kernel,
        out_shape=(
            jax.ShapeDtypeStruct((SHARE, CAND), jnp.float32),
            jax.ShapeDtypeStruct((SHARE, CAND), jnp.float32),
            jax.ShapeDtypeStruct((NB, 8, SHARE), jnp.float32),
        ),
        in_specs=[
            pl.BlockSpec(memory_space=pltpu.SMEM),
            pl.BlockSpec(memory_space=pltpu.VMEM),
            pl.BlockSpec(memory_space=pl.ANY),
        ],
        scratch_shapes=[
            pltpu.VMEM((PER_X, QBLK, LANES), jnp.bfloat16),
            pltpu.SemaphoreType.DMA,
        ],
        compiler_params=pltpu.CompilerParams(vmem_limit_bytes=8 << 20),
        cost_estimate=pl.CostEstimate(
            flops=12 * SHARE * CAND, bytes_accessed=20 * SHARE * CAND, transcendentals=SHARE * CAND
        ),
        name="column_stats",
    )(at, parts, in_hbm(q_all))


def weigh_kernel(s_ref, hit_ref, stat_ref, w_ref):
    tops, totals, picked = stat_ref[:, 0, :], stat_ref[:, 1, :], stat_ref[:, 2, :]
    top = jnp.max(tops, axis=0, keepdims=True)
    total = jnp.sum(totals * jnp.exp(tops - top), axis=0, keepdims=True)
    losses = top + jnp.log(total) - jnp.sum(picked, axis=0, keepdims=True)
    row = lax.broadcasted_iota(jnp.int32, (LANES, SHARE), 0)
    turned = jnp.where(row == 0, top, jnp.where(row == 1, total, 0.0)).T
    probs = jnp.exp(s_ref[...] - turned[:, :1]) / turned[:, 1:2]
    weights = (probs - hit_ref[...]).astype(jnp.bfloat16)
    loss = jnp.sum(losses, axis=1, keepdims=True)
    first = loss.astype(jnp.bfloat16).astype(jnp.float32)
    second = (loss - first).astype(jnp.bfloat16).astype(jnp.float32)
    row = lax.broadcasted_iota(jnp.int32, (SENT - SHARE, LANES), 0)
    pieces = jnp.where(row == 1, second, jnp.where(row == 2, loss - first - second, 0.0))
    pieces = jnp.where(row == 0, first, pieces).astype(jnp.bfloat16)
    for h in range(HALVES):
        w_ref[h, :SHARE] = weights[:, h * LANES : (h + 1) * LANES]
        w_ref[h, SHARE:] = pieces


def weigh(scores, hits, stats):
    return pl.pallas_call(
        weigh_kernel,
        out_shape=jax.ShapeDtypeStruct((HALVES, SENT, LANES), jnp.bfloat16),
        compiler_params=pltpu.CompilerParams(vmem_limit_bytes=8 << 20),
        cost_estimate=pl.CostEstimate(
            flops=10 * SHARE * CAND, bytes_accessed=6 * SHARE * CAND, transcendentals=SHARE * CAND
        ),
        name="weigh",
    )(scores, hits, stats)


def block_weights(w_ref, b):
    start = pl.multiple_of(lax.rem(b, PER_X) * QBLK, QBLK)
    slab = lax.div(b, PER_X) * HALVES
    return jnp.concatenate([w_ref[slab + h, pl.ds(start, QBLK), :] for h in range(HALVES)], axis=1)


def passage_kernel(sel_ref, q_ref, w_ref, pg_ref, kept_ref, acc, sems):
    width = acc.shape[1]
    keep = pltpu.make_async_copy(w_ref, kept_ref, sems.at[NZ])
    keep.start()
    acc[...] = jnp.zeros_like(acc)

    def add(b, part, done):
        cand = lax.dot_general(
            w_ref[b // PER_X * HALVES + part, b % PER_X * QBLK : (b % PER_X + 1) * QBLK],
            q_ref[b][:, :width],
            (((0,), (0,)), ((), ())),
            preferred_element_type=jnp.float32,
        )
        for k in range(NZ // 2):
            z = part * (NZ // 2) + k
            start = pl.multiple_of(z * GROUP + sel_ref[z, b] * PBLK, PBLK)
            acc[pl.ds(start, PBLK), :] += cand[k * PBLK : (k + 1) * PBLK, :]
            done(z)

    def send(z):
        at = pl.ds(z * GROUP, GROUP)
        return pltpu.make_async_copy(acc.at[at], pg_ref.at[at], sems.at[z])

    for part in range(2):
        for b in range(NB - 1):
            add(b, part, lambda z: None)
        add(NB - 1, part, lambda z: send(z).start())
    for z in range(NZ):
        send(z).wait()
    keep.wait()


def passage_part(sel, q_all, weights):
    width = q_all.shape[2] - LANES
    whole = pl.BlockSpec(memory_space=pltpu.VMEM)
    apart = pl.BlockSpec(memory_space=pl.ANY)
    return pl.pallas_call(
        passage_kernel,
        out_shape=(
            pltpu.HBM((NZ * GROUP, width), jnp.float32),
            pltpu.HBM(weights.shape, weights.dtype),
        ),
        grid_spec=pltpu.PrefetchScalarGridSpec(
            num_scalar_prefetch=1,
            grid=(),
            in_specs=[whole, whole],
            out_specs=(apart, apart),
            scratch_shapes=[
                pltpu.VMEM((NZ * GROUP, width), jnp.float32),
                pltpu.SemaphoreType.DMA((NZ + 1,)),
            ],
        ),
        compiler_params=pltpu.CompilerParams(vmem_limit_bytes=16 << 20),
        cost_estimate=pl.CostEstimate(
            flops=2 * NB * QBLK * CAND * width,
            bytes_accessed=(2 * NB * QBLK + 4 * NZ * GROUP) * width + 2 * NB * QBLK * CAND,
            transcendentals=0,
        ),
        name="passage_part",
    )(sel, q_all, weights)


def query_kernel(sel_ref, tab_ref, p_ref, w_ref, *rest):
    *arrived, qg_ref, chosen = rest
    b = tab_ref[pl.program_id(0)]
    pick_rows(sel_ref, p_ref, chosen, b)
    share = jnp.dot(block_weights(w_ref, b), chosen[...], preferred_element_type=jnp.float32)
    qg_ref[0] = share + arrived[0][0] if arrived else share


def query_part(sel, tab, p_all, weights, *arrived):
    width = p_all.shape[1]
    block = pl.BlockSpec((1, QBLK, width), lambda k, sel, tab: (k, 0, 0))
    return pl.pallas_call(
        query_kernel,
        out_shape=jax.ShapeDtypeStruct((NY, QBLK, width), jnp.float32),
        grid_spec=pltpu.PrefetchScalarGridSpec(
            num_scalar_prefetch=2,
            grid=(NY,),
            in_specs=[
                pl.BlockSpec((NZ * GROUP, width), lambda k, sel, tab: (0, 0)),
                pl.BlockSpec((NX * HALVES, SENT, LANES), lambda k, sel, tab: (0, 0, 0)),
            ]
            + [block] * len(arrived),
            out_specs=block,
            scratch_shapes=[pltpu.VMEM((CAND, width), jnp.bfloat16)],
        ),
        compiler_params=pltpu.CompilerParams(vmem_limit_bytes=16 << 20),
        cost_estimate=pl.CostEstimate(
            flops=2 * NY * QBLK * CAND * width,
            bytes_accessed=(4 * NY * QBLK + 2 * NZ * GROUP) * width + 2 * NB * QBLK * CAND,
            transcendentals=0,
        ),
        name="query_part",
    )(sel, tab, in_hbm(p_all), in_hbm(weights), *arrived)


def total_over(value, axis, size):
    copies = jnp.broadcast_to(value[None], (size,) + value.shape)
    return jnp.sum(lax.all_to_all(copies, axis, split_axis=0, concat_axis=0, tiled=True), axis=0)


def per_device(queries, passages, pair_block, positives):
    z, core, x = lax.axis_index("z"), lax.axis_index("core"), lax.axis_index("x")
    width = queries.shape[1]
    at = jnp.stack([lax.axis_index("y") * NC + core, x, z * NB]).astype(jnp.int32)
    code, marked = encode(passages, pair_block, queries, positives)
    q_all = lax.all_gather(marked, COL, axis=0, tiled=False)
    coded = lax.all_gather(code, "z", axis=0, tiled=True).astype(jnp.bfloat16)
    coded = coded.reshape(NZ, *code.shape)
    part, p_all, sel = partial_scores(at, q_all, coded)
    parts = lax.all_to_all(
        part.reshape(NX, SHARE, CAND), "x", split_axis=0, concat_axis=0, tiled=True
    )
    scores, hits, stats = column_stats(at, parts, q_all)
    stats = lax.all_to_all(stats, COL, split_axis=0, concat_axis=0, tiled=True)
    weights = lax.all_gather(weigh(scores, hits, stats), "x", axis=0, tiled=True)
    loss = jnp.sum(weights[::HALVES, SHARE : SHARE + 3, :1].astype(jnp.float32))

    passages_part, weights = passage_part(sel, q_all, weights)
    passage_grad = lax.psum_scatter(passages_part, "z", scatter_dimension=0, tiled=True)
    mine = jnp.arange(NY, dtype=jnp.int32) * NC + core
    away = jnp.arange(NY, dtype=jnp.int32) * NC + (1 - core)
    arrived = lax.ppermute(query_part(sel, away, p_all, weights), "core", [(0, 1), (1, 0)])
    query_grad = jnp.sum(
        lax.all_to_all(
            query_part(sel, mine, p_all, weights, arrived),
            "y",
            split_axis=0,
            concat_axis=0,
            tiled=True,
        ),
        axis=0,
    )
    loss = total_over(jnp.full((8, LANES), loss), "z", NZ)[0, 0] / QUERIES
    return loss, query_grad, passage_grad


def solution(mesh):
    fine = Mesh(mesh.devices.reshape(NZ, NY, NC, NX), DP + ("x",))
    in_specs = (P(DP, "x"), P(DP, "x"), P(None, DP), P(DP))
    out_specs = (P(), P(DP, "x"), P(DP, "x"))
    return jax.shard_map(
        per_device, mesh=fine, in_specs=in_specs, out_specs=out_specs, check_vma=False
    )
```
